256 devices in a mesh: member: 32 (over y, z_lo, core), tensor: 8 (over x, z_hi).
Axes of the slice: x: 4, y: 4, z: 8 (z_hi: 2, z_lo: 4; z = z_hi * 4 + z_lo), core: 2. Of those that a mesh axis runs over, the one named last changes fastest.
Arguments:
- prompt_states: bfloat16 [16384, 5120], P('member', 'tensor'), may hold values from -6 to 6
- decode_states: bfloat16 [8192, 5120], P('member', 'tensor'), may hold values from -6 to 6
- norm_gain: bfloat16 [5120], P('tensor'), may hold values from 0.5 to 7, as said below
- query_bias: bfloat16 [5120], P('tensor'), may hold values from -3 to 3
- value_bias: bfloat16 [1024], P('tensor'), may hold values from -3 to 3
- w_query: bfloat16 [5120, 5120], P('member', 'tensor'), may hold values from -0.078125 to 0.078125
- w_key: bfloat16 [5120, 1024], P('member', 'tensor'), may hold values from -0.078125 to 0.078125
- w_value: bfloat16 [5120, 1024], P('member', 'tensor'), may hold values from -0.078125 to 0.078125
- w_out: bfloat16 [5120, 5120], P('tensor', 'member'), may hold values from -0.078125 to 0.078125
- targets: bfloat16 [8192, 5120], P('member', 'tensor'), may hold values from -3 to 3
- lengths: int32 [64], replicated, may hold values from 1 to 128, 4096 in all
- seeds: int32 [32], replicated, may hold values from 0 to 46336
Outputs:
- fitness: float32 [64], replicated
- grad_query: float32 [5120, 5120], P('member', 'tensor')
- grad_key: float32 [5120, 1024], P('member', 'tensor')
- grad_value: float32 [5120, 1024], P('member', 'tensor')
- grad_out: float32 [5120, 5120], P('tensor', 'member')
The draws below stay inside these ranges and needn't reach their ends.
Inputs may be any that keep to these rules, and one draw needn't show every extreme that they name: lengths[2 m] and lengths[2 m + 1] belong to pair m; all lengths sum to exactly 4096, and one of them equals 128. `norm_gain`: positive gains.
All inputs are finite; a program needn't handle non-finite values.
Results may differ from the reference program's by a relative error of at most 0.018.
The reference program's roundings to bfloat16 on the way count: a program that leaves them out, or rounds other values in their place, can miss the bound.
Values may be sent and summed in bfloat16 or wider, within the bound.
No kernel may reach another device: no remote copies, remote signals or barrier semaphores. Data moves between devices by JAX's collectives and lax.ppermute only.
A program may use at most 128 MiB of HBM per device.

```python
import math
import jax
import jax.numpy as jnp
import numpy as np
from jax import lax

D = 5120
HEADS = 40
KV_HEADS = 8
HEAD_DIM = 128
PROMPT = 512
DEC = 128
RANK = 16
POP = 64
PROMPT_ROWS = 16384
DECODE_ROWS = 8192
N_MEMBER = 32
N_TENSOR = 8


def draw_norm_gain(key, part):
    values = 1.0 + 0.15 * jax.random.normal(key, (D,), jnp.float32)
    return jnp.clip(values, 0.5, 1.5).astype(jnp.bfloat16)


def plant(array, stream_key, smallest, largest):
    longest = array.shape.index(max(array.shape))
    spots = []
    for shift in (0, 1):
        where = [jax.random.randint(jax.random.fold_in(stream_key, axis), (), 0, length) for axis, length in enumerate(array.shape)]
        where[longest] = (where[longest] + shift) % array.shape[longest]
        spots.append(tuple(where))
    return array.at[spots[0]].set(smallest).at[spots[1]].set(largest)


def level_of(own_key, shape, cuts, low, high):
    def one(axis_at, shards_of):
        draws = jax.random.uniform(jax.random.fold_in(jax.random.fold_in(own_key, 6), axis_at), (shards_of,), jnp.float32, low / len(cuts), high / len(cuts))
        return jnp.repeat(jnp.exp(draws), shape[axis_at] // shards_of).reshape((-1,) + (1,) * (len(shape) - axis_at - 1))

    loudness = one(*cuts[0])
    for cut in cuts[1:]:
        loudness = loudness * one(*cut)
    return loudness


def length_profile(number_of, total, reach, lean):
    weights = [(1 << 20) // math.isqrt(grade ** lean) + 1 for grade in range(2, number_of + 1)]
    spare, counts = total - reach - (number_of - 1), [1] * (number_of - 1)
    while spare > 0:
        free = [i for i in range(number_of - 1) if counts[i] < reach]
        pool, budget = sum([weights[i] for i in free]), spare
        for i in free:
            addition = min(reach - counts[i], max(1, budget * weights[i] // pool), spare)
            counts[i] = counts[i] + addition
            spare = spare - addition
    return np.array([reach] + counts)


def uneven(stream_key, number_of, total, most, skew):
    if number_of == 2:
        one = jax.random.randint(stream_key, (), max(1, total - most), min(most, total - 1) + 1)
        return jnp.stack([one, total - one])
    sizes = jnp.asarray(length_profile(number_of, total, most, skew), jnp.int32)
    couples = (number_of - 1) // 2
    donor, sink = sizes[1:1 + 2 * couples:2], sizes[2:2 + 2 * couples:2]
    slack = jnp.minimum(donor - 1, most - sink)
    shifted = jax.random.randint(jax.random.fold_in(stream_key, 1), (couples,), 0, 1 << 20) % (slack + 1)
    sizes = sizes.at[1:1 + 2 * couples:2].set(donor - shifted).at[2:2 + 2 * couples:2].set(sink + shifted)
    return sizes[jax.random.permutation(jax.random.fold_in(stream_key, 2), number_of)]


def centred(rng, dims, deviation, reach, cuts=(), held_as=jnp.bfloat16):
    entries = jax.random.normal(rng, dims, jnp.float32) * deviation
    if len(cuts) > 0:
        entries = level_of(rng, dims, cuts, -0.22, 0.18) * entries
    return jnp.clip(entries, min=-reach, max=reach).astype(held_as)


def setup_inputs(seed: int = 0) -> dict:
    streams_of = jax.random.split(jax.random.key(seed), 13)
    return {
        "prompt_states": centred(streams_of[0], (PROMPT_ROWS, D), 1.0, 6.0, ((0, 32), (1, 8))),
        "decode_states": centred(streams_of[1], (DECODE_ROWS, D), 1.0, 6.0, ((0, 32), (1, 8))),
        "norm_gain": draw_norm_gain(jax.random.fold_in(streams_of[12], 71), 0),
        "query_bias": centred(streams_of[3], (HEADS * HEAD_DIM,), 0.5, 3.0, ((0, 8),)),
        "value_bias": centred(streams_of[4], (KV_HEADS * HEAD_DIM,), 0.5, 3.0, ((0, 8),)),
        "w_query": centred(streams_of[5], (D, HEADS * HEAD_DIM), D ** -0.5, 0.078125, ((0, 32), (1, 8))),
        "w_key": centred(streams_of[6], (D, KV_HEADS * HEAD_DIM), D ** -0.5, 0.078125, ((0, 32), (1, 8))),
        "w_value": centred(streams_of[7], (D, KV_HEADS * HEAD_DIM), D ** -0.5, 0.078125, ((0, 32), (1, 8))),
        "w_out": centred(streams_of[8], (HEADS * HEAD_DIM, D), (HEADS * HEAD_DIM) ** -0.5, 0.078125, ((0, 8), (1, 32))),
        "targets": centred(streams_of[9], (DECODE_ROWS, D), 0.5, 3.0, ((0, 32), (1, 8))),
        "lengths": uneven(streams_of[10], POP, N_MEMBER * DEC, DEC, 2).astype(jnp.int32),
        "seeds": plant(jax.random.randint(streams_of[11], (N_MEMBER,), 0, 46337), jax.random.fold_in(streams_of[11], 1), 0, 46336).astype(jnp.int32),
    }


PRIME = 46337
SIGMA_SCALE = 0.3
NEG_LARGE = -1e+30

def noise_table(seed_value, matrix_id, positions, rank_count):
    rank_ids = jnp.arange(rank_count, dtype=jnp.int32)
    mixing_matrix = (seed_value + (matrix_id * rank_count + rank_ids)[None, :] * 2749 + positions[:, None] * 6271) % PRIME
    hashed = (mixing_matrix * mixing_matrix + 1013) % PRIME
    hashed = (hashed * hashed + mixing_matrix) % PRIME
    hashed = (hashed * hashed + 1013) % PRIME
    return ((hashed.astype(jnp.float32) * (2.0 / PRIME) - 1.0) * math.sqrt(3.0)).astype(jnp.bfloat16)

def normed(states, gain):
    values = states.astype(jnp.float32)
    scale = lax.rsqrt(lax.optimization_barrier(jnp.mean(values * values, axis=-1, keepdims=True)) + 1e-06)
    return (values * scale * gain.astype(jnp.float32)).astype(jnp.bfloat16)

def low_term(left_factor, table_a, table_b):
    inner = jnp.dot(left_factor, table_a, preferred_element_type=jnp.float32)
    return jnp.dot(inner, table_b.astype(jnp.float32).T, precision=lax.Precision.HIGHEST)

def attend(query, keys, values, group, head_dim, prompt_len):
    count = query.shape[0]
    kv_count = keys.shape[1] // head_dim
    query_four = query.astype(jnp.float32).reshape(count, kv_count, group, head_dim)
    keys_three = keys.astype(jnp.float32).reshape(-1, kv_count, head_dim)
    values_three = values.astype(jnp.float32).reshape(-1, kv_count, head_dim)
    scores = jnp.einsum('pkgd,nkd->kgpn', query_four, keys_three) / math.sqrt(head_dim)
    key_index = jnp.arange(keys_three.shape[0], dtype=jnp.int32) - prompt_len
    query_index = jnp.arange(count, dtype=jnp.int32)
    allowed = key_index[None, :] <= query_index[:, None]
    scores = jnp.where(allowed, scores, NEG_LARGE)
    top = lax.optimization_barrier(jnp.max(scores, axis=-1, keepdims=True))
    exponent = jnp.exp(scores - top)
    weights = (exponent / lax.optimization_barrier(jnp.sum(exponent, axis=-1, keepdims=True))).astype(jnp.bfloat16)
    mixed = jnp.einsum('kgpn,nkd->pkgd', weights.astype(jnp.float32), values_three)
    return mixed.astype(jnp.bfloat16).reshape(count, kv_count * group * head_dim)

def reference(prompt_states, decode_states, norm_gain, query_bias, value_bias, w_query, w_key, w_value, w_out, targets, lengths, seeds):
    sigma = SIGMA_SCALE / math.sqrt(D)
    lift = sigma / math.sqrt(RANK)
    group = HEADS // KV_HEADS
    share_width = HEADS * HEAD_DIM // N_TENSOR
    row_ids = jnp.arange(D, dtype=jnp.int32)
    query_cols = jnp.arange(HEADS * HEAD_DIM, dtype=jnp.int32)
    pair_cols = jnp.arange(KV_HEADS * HEAD_DIM, dtype=jnp.int32)

    def member_fitness(member):
        seed_value = seeds[member]
        prompt_rows = lax.dynamic_slice_in_dim(prompt_states, member * PROMPT, PROMPT, 0)
        decode_rows = lax.dynamic_slice_in_dim(decode_states, member * 2 * DEC, 2 * DEC, 0)
        goal = lax.dynamic_slice_in_dim(targets, member * 2 * DEC, 2 * DEC, 0).astype(jnp.float32)
        prompt_normed = normed(prompt_rows, norm_gain)
        decode_normed = normed(decode_rows, norm_gain)
        a_query = noise_table(seed_value, 0, row_ids, RANK)
        a_key = noise_table(seed_value, 1, row_ids, RANK)
        a_value = noise_table(seed_value, 2, row_ids, RANK)
        a_out = noise_table(seed_value, 3, query_cols, RANK)
        b_query = noise_table(seed_value, 4, query_cols, RANK)
        b_key = noise_table(seed_value, 5, pair_cols, RANK)
        b_value = noise_table(seed_value, 6, pair_cols, RANK)
        b_out = noise_table(seed_value, 7, row_ids, RANK)
        prompt_key_base = jnp.dot(prompt_normed, w_key, preferred_element_type=jnp.float32)
        prompt_value_base = jnp.dot(prompt_normed, w_value, preferred_element_type=jnp.float32)
        low_prompt_key = low_term(prompt_normed, a_key, b_key)
        low_prompt_value = low_term(prompt_normed, a_value, b_value)
        query_base = jnp.dot(decode_normed, w_query, preferred_element_type=jnp.float32)
        key_base = jnp.dot(decode_normed, w_key, preferred_element_type=jnp.float32)
        value_base = jnp.dot(decode_normed, w_value, preferred_element_type=jnp.float32)
        low_query = low_term(decode_normed, a_query, b_query)
        low_key = low_term(decode_normed, a_key, b_key)
        low_value = low_term(decode_normed, a_value, b_value)
        results = []
        for sign_index in range(2):
            sign = 1.0 - 2.0 * sign_index
            first = sign_index * DEC
            last = first + DEC
            prompt_key = (prompt_key_base + sign * lift * low_prompt_key).astype(jnp.bfloat16)
            prompt_value = (prompt_value_base + value_bias.astype(jnp.float32) + sign * lift * low_prompt_value).astype(jnp.bfloat16)
            query = (query_base[first:last] + query_bias.astype(jnp.float32) + sign * lift * low_query[first:last]).astype(jnp.bfloat16)
            key = (key_base[first:last] + sign * lift * low_key[first:last]).astype(jnp.bfloat16)
            value = (value_base[first:last] + value_bias.astype(jnp.float32) + sign * lift * low_value[first:last]).astype(jnp.bfloat16)
            mixed = attend(query, jnp.concatenate([prompt_key, key], axis=0), jnp.concatenate([prompt_value, value], axis=0), group, HEAD_DIM, PROMPT)
            output = jnp.zeros((DEC, D), jnp.float32)
            for share in range(N_TENSOR):
                low_col = share * share_width
                high_col = low_col + share_width
                mixed_share = mixed[:, low_col:high_col]
                partial_value = jnp.dot(mixed_share, w_out[low_col:high_col], preferred_element_type=jnp.float32) + sign * lift * low_term(mixed_share, a_out[low_col:high_col], b_out)
                rounded = lax.optimization_barrier(partial_value.astype(jnp.bfloat16))
                output = output + rounded.astype(jnp.float32)
            difference = output - goal[first:last]
            fitness_errors = lax.optimization_barrier(jnp.sum(difference * difference, axis=1)) / D
            length = lengths[2 * member + sign_index]
            live = jnp.arange(DEC, dtype=jnp.int32) < length
            results.append(-jnp.sum(jnp.where(live, fitness_errors, 0.0)) / length.astype(jnp.float32))
        return jnp.stack(results)
    fitness = lax.map(member_fitness, jnp.arange(N_MEMBER, dtype=jnp.int32)).reshape(2 * N_MEMBER)
    differences = fitness[0::2] - fitness[1::2]
    factor = 1.0 / (2.0 * N_MEMBER * sigma * math.sqrt(RANK))
    row_of_weights = differences * factor

    def update(first_id, second_id, left_ids, right_ids):
        left_factor = jax.vmap(lambda seed_one: noise_table(seed_one, first_id, left_ids, RANK))(seeds).astype(jnp.float32)
        right_factor = jax.vmap(lambda seed_one: noise_table(seed_one, second_id, right_ids, RANK))(seeds).astype(jnp.float32)
        return jnp.einsum('lqh,lah->qa', left_factor * row_of_weights[:, None, None], right_factor, precision=lax.Precision.HIGHEST)
    grad_query = update(0, 4, row_ids, query_cols)
    grad_key = update(1, 5, row_ids, pair_cols)
    grad_value = update(2, 6, row_ids, pair_cols)
    grad_out = update(3, 7, query_cols, row_ids)
    return (fitness, grad_query, grad_key, grad_value, grad_out)
```

```python
import functools
import math

import jax
import jax.numpy as jnp
import numpy as np
from jax import lax
from jax.experimental import pallas as pl
from jax.experimental.pallas import tpu as pltpu
from jax.sharding import Mesh
from jax.sharding import PartitionSpec as P

D = 5120
HEADS = 40
KV_HEADS = 8
HEAD_DIM = 128
PROMPT = 512
DEC = 128
RANK = 16
N_MEMBER = 32
N_TENSOR = 8
GROUP = HEADS // KV_HEADS
SHARE = D // N_TENSOR
PIECE = D // N_MEMBER
QUERY_WIDTH = HEADS * HEAD_DIM // N_TENSOR
ALL_WIDTH = QUERY_WIDTH + 2 * HEAD_DIM
ROWS = 2 * DEC + PROMPT
PAD = 16
KDIM = N_MEMBER * RANK

PRIME = 46337
SIGMA = 0.3 / math.sqrt(D)
LIFT = SIGMA / math.sqrt(RANK)
FACTOR = 1.0 / (2.0 * N_MEMBER * SIGMA * math.sqrt(RANK))
NEG_LARGE = -1e30

MEMBER = ("y", "l", "c")
TENSOR = ("x", "h")
F32 = jnp.float32
BF16 = jnp.bfloat16


def modulo(value):
    quotient = (value.astype(F32) * (1.0 / PRIME)).astype(jnp.int32)
    rest = value - quotient * PRIME
    rest = jnp.where(rest < 0, rest + PRIME, rest)
    return jnp.where(rest >= PRIME, rest - PRIME, rest)


def noise(mixing):
    mixing = modulo(mixing)
    hashed = modulo(mixing * mixing + 1013)
    hashed = modulo(hashed * hashed + mixing)
    hashed = modulo(hashed * hashed + 1013)
    return ((hashed.astype(F32) * (2.0 / PRIME) - 1.0) * math.sqrt(3.0)).astype(BF16)


def tall_table(seed, first, count, positions, width):
    columns = jnp.arange(width, dtype=jnp.int32)
    values = noise(seed + (first * RANK + columns)[None, :] * 2749 + positions[:, None] * 6271)
    return jnp.where((columns < count * RANK)[None, :], values, jnp.zeros((), BF16))


def wide_table(seed, matrix, positions):
    ranks = jnp.arange(RANK, dtype=jnp.int32)
    return noise(seed + (matrix * RANK + ranks)[:, None] * 2749 + positions[None, :] * 6271)


def all_left(seeds, matrix, positions):
    ranks = jnp.arange(RANK, dtype=jnp.int32)
    base = (seeds[:, None] + (matrix * RANK + ranks)[None, :] * 2749).reshape(1, KDIM)
    return noise(base + positions[:, None] * 6271)


def all_right(seeds, matrix, positions):
    ranks = jnp.arange(RANK, dtype=jnp.int32)
    base = (seeds[:, None] + (matrix * RANK + ranks)[None, :] * 2749).reshape(KDIM, 1)
    return noise(base + positions[None, :] * 6271)


def split_dot(left, right):
    high = left.astype(BF16)
    low = (left - high.astype(F32)).astype(BF16)
    return jnp.dot(high, right, preferred_element_type=F32) + jnp.dot(
        low, right, preferred_element_type=F32
    )


def nt_dot(left, right):
    return lax.dot_general(left, right, (((1,), (1,)), ((), ())), preferred_element_type=F32)


def attention_kernel(
    order,
    scale,
    query_bias,
    value_bias,
    table_right,
    table_left,
    weights,
    a0, a1, a2, a3u, a3d,
    b0, b1, b2, b3u, b3d,
    mixed,
    held,
    sems,
):
    copies = []
    for i in range(N_TENSOR):
        rows = pl.ds(pl.multiple_of(order[i] * SHARE, SHARE), SHARE)
        copy = pltpu.make_async_copy(weights.at[rows], held.at[i], sems.at[i])
        copy.start()
        copies.append(copy)
    row_scale = scale[...]
    query = jnp.zeros((2 * DEC, QUERY_WIDTH), F32)
    pair = jnp.zeros((ROWS, 2 * HEAD_DIM), F32)
    inner = jnp.zeros((ROWS, HEAD_DIM), F32)
    half = 384
    for i, piece in enumerate((a0, b0, a1, a2, b1, b2, (a3u, a3d), (b3u, b3d))):
        if isinstance(piece, tuple):
            raw = jnp.concatenate([piece[0][...], piece[1][: ROWS - half]], axis=0)
            gain = piece[1][ROWS - half : ROWS - half + 1]
        else:
            raw = piece[:ROWS]
            gain = piece[ROWS : ROWS + 1]
        normed = (raw.astype(F32) * row_scale * gain.astype(F32)).astype(BF16)
        rows = pl.ds(pl.multiple_of(order[i] * SHARE, SHARE), SHARE)
        inner += jnp.dot(normed, table_left[rows, :], preferred_element_type=F32)
        copies[i].wait()
        query += jnp.dot(normed[: 2 * DEC], held[i, :, :QUERY_WIDTH], preferred_element_type=F32)
        pair += jnp.dot(normed, held[i, :, QUERY_WIDTH:], preferred_element_type=F32)
    inner = inner * LIFT
    low_decode = split_dot(inner[: 2 * DEC], table_right[...])
    low_prompt = split_dot(inner[2 * DEC :], table_right[:, QUERY_WIDTH:])
    bias_q = query_bias[...].astype(F32)
    bias_v = value_bias[...].astype(F32)
    causal = lax.broadcasted_iota(jnp.int32, (DEC, DEC), 1) <= lax.broadcasted_iota(
        jnp.int32, (DEC, DEC), 0
    )
    for s in range(2):
        sign = 1.0 - 2.0 * s
        own = slice(s * DEC, (s + 1) * DEC)
        low = sign * low_decode[own]
        q = (query[own] + bias_q + low[:, :QUERY_WIDTH]).astype(BF16)
        k_own = (pair[own, :HEAD_DIM] + low[:, QUERY_WIDTH : QUERY_WIDTH + HEAD_DIM]).astype(BF16)
        v_own = (pair[own, HEAD_DIM:] + bias_v + low[:, QUERY_WIDTH + HEAD_DIM :]).astype(BF16)
        k_prompt = (pair[2 * DEC :, :HEAD_DIM] + sign * low_prompt[:, :HEAD_DIM]).astype(BF16)
        v_prompt = (pair[2 * DEC :, HEAD_DIM:] + bias_v + sign * low_prompt[:, HEAD_DIM:]).astype(
            BF16
        )
        for head in range(GROUP):
            cols = slice(head * HEAD_DIM, (head + 1) * HEAD_DIM)
            far = nt_dot(q[:, cols], k_prompt) * (1.0 / math.sqrt(HEAD_DIM))
            near = nt_dot(q[:, cols], k_own) * (1.0 / math.sqrt(HEAD_DIM))
            near = jnp.where(causal, near, NEG_LARGE)
            top = jnp.maximum(
                jnp.max(far, axis=1, keepdims=True), jnp.max(near, axis=1, keepdims=True)
            )
            far = jnp.exp(far - top)
            near = jnp.exp(near - top)
            total = jnp.sum(far, axis=1, keepdims=True) + jnp.sum(near, axis=1, keepdims=True)
            far = (far / total).astype(BF16)
            near = (near / total).astype(BF16)
            mixed[own, cols] = (
                jnp.dot(far, v_prompt, preferred_element_type=F32)
                + jnp.dot(near, v_own, preferred_element_type=F32)
            ).astype(BF16)


def attention(order, scale, query_bias, value_bias, table_right, table_left, weights, pieces):
    vmem = pl.BlockSpec(memory_space=pltpu.VMEM)
    return pl.pallas_call(
        attention_kernel,
        out_shape=jax.ShapeDtypeStruct((2 * DEC, QUERY_WIDTH), BF16),
        in_specs=[pl.BlockSpec(memory_space=pltpu.SMEM)]
        + [vmem] * 5
        + [pl.BlockSpec(memory_space=pl.ANY)]
        + [vmem] * len(pieces),
        out_specs=vmem,
        scratch_shapes=[
            pltpu.VMEM((N_TENSOR, SHARE, ALL_WIDTH), BF16),
            pltpu.SemaphoreType.DMA((N_TENSOR,)),
        ],
        compiler_params=pltpu.CompilerParams(vmem_limit_bytes=56 * 1024 * 1024),
        cost_estimate=pl.CostEstimate(
            flops=5_200_000_000, bytes_accessed=20_000_000, transcendentals=820_000
        ),
    )(order, scale, query_bias, value_bias, table_right, table_left, weights, *pieces)


def output_kernel(
    order,
    place,
    weights,
    table_left,
    table_right,
    targets,
    a0, a1, a2, a3u, a3d,
    b0, b1, b2, b3u, b3d,
    result,
    held,
    sems,
):
    copies = []
    for i in range(N_TENSOR):
        rows = pl.ds(pl.multiple_of(order[i] * SHARE, SHARE), SHARE)
        copy = pltpu.make_async_copy(weights.at[rows], held.at[i], sems.at[i])
        copy.start()
        copies.append(copy)
    row = lax.broadcasted_iota(jnp.int32, (2 * DEC, 1), 0)
    lifts = jnp.where(row < DEC, LIFT, -LIFT).astype(F32)
    total = jnp.zeros((2 * DEC, SHARE), F32)
    for i, piece in enumerate((a0, b0, a1, a2, b1, b2, (a3u, a3d), (b3u, b3d))):
        if isinstance(piece, tuple):
            share = jnp.concatenate([piece[0][...], piece[1][...]], axis=0)
        else:
            share = piece[...]
        rows = pl.ds(pl.multiple_of(order[i] * SHARE, SHARE), SHARE)
        inner = jnp.dot(share, table_left[rows, :], preferred_element_type=F32) * lifts
        copies[i].wait()
        partial = nt_dot(share, held[i]) + split_dot(inner, table_right[...])
        total += partial.astype(BF16).astype(F32)
    difference = total - targets[...].astype(F32)
    errors = jnp.sum(difference * difference, axis=1, keepdims=True) * (1.0 / D)
    lane = lax.broadcasted_iota(jnp.int32, (N_TENSOR, 128), 1)
    line = lax.broadcasted_iota(jnp.int32, (N_TENSOR, 128), 0)
    member, tensor = place[0], place[1]
    found = jnp.zeros((N_TENSOR, 128), F32)
    for s in range(2):
        length = place[2 + s]
        live = lax.broadcasted_iota(jnp.int32, (DEC, 1), 0) < length
        summed = jnp.sum(
            jnp.where(live, errors[s * DEC : (s + 1) * DEC], 0.0), axis=0, keepdims=True
        )
        lengths = jnp.full((1, 1), length, jnp.int32).astype(F32)
        mine = (line == tensor) & (lane == 2 * member + s)
        found = jnp.where(mine, -(summed / lengths), found)
    result[...] = found


def output_errors(order, place, weights, table_left, table_right, targets, pieces):
    vmem = pl.BlockSpec(memory_space=pltpu.VMEM)
    smem = pl.BlockSpec(memory_space=pltpu.SMEM)
    return pl.pallas_call(
        output_kernel,
        out_shape=jax.ShapeDtypeStruct((N_TENSOR, 128), F32),
        in_specs=[smem, smem, pl.BlockSpec(memory_space=pl.ANY)] + [vmem] * (3 + len(pieces)),
        out_specs=vmem,
        scratch_shapes=[
            pltpu.VMEM((N_TENSOR, SHARE, QUERY_WIDTH), BF16),
            pltpu.SemaphoreType.DMA((N_TENSOR,)),
        ],
        compiler_params=pltpu.CompilerParams(vmem_limit_bytes=56 * 1024 * 1024),
        cost_estimate=pl.CostEstimate(
            flops=2_200_000_000, bytes_accessed=12_000_000, transcendentals=0
        ),
    )(order, place, weights, table_left, table_right, targets, *pieces)


def gradient_kernel(gathered, lq, rq, lk, rk, lv, rv, lo, ro, fitness, gq, gk, gv, go):
    values = jnp.sum(gathered[...], axis=0, keepdims=True)
    fitness[...] = values
    lane = lax.broadcasted_iota(jnp.int32, (128, 128), 1)
    line = lax.broadcasted_iota(jnp.int32, (128, 128), 0)
    column = jnp.sum(jnp.where(lane == line, values, 0.0), axis=1, keepdims=True)
    entry = lax.broadcasted_iota(jnp.int32, (128, KDIM), 0)
    pair = lax.broadcasted_iota(jnp.int32, (128, KDIM), 1) // RANK
    signed = jnp.where(entry == 2 * pair, column, 0.0) - jnp.where(
        entry == 2 * pair + 1, column, 0.0
    )
    weights = jnp.sum(signed, axis=0, keepdims=True) * FACTOR
    for left, right, grad in ((lq, rq, gq), (lk, rk, gk), (lv, rv, gv), (lo, ro, go)):
        grad[...] = split_dot(left[...].astype(F32) * weights, right[...])


def gradients(gathered, factors):
    vmem = pl.BlockSpec(memory_space=pltpu.VMEM)
    return pl.pallas_call(
        gradient_kernel,
        out_shape=(
            jax.ShapeDtypeStruct((1, 128), F32),
            jax.ShapeDtypeStruct((PIECE, QUERY_WIDTH), F32),
            jax.ShapeDtypeStruct((PIECE, HEAD_DIM), F32),
            jax.ShapeDtypeStruct((PIECE, HEAD_DIM), F32),
            jax.ShapeDtypeStruct((QUERY_WIDTH, PIECE), F32),
        ),
        in_specs=[vmem] * 9,
        out_specs=(vmem,) * 5,
        compiler_params=pltpu.CompilerParams(vmem_limit_bytes=40 * 1024 * 1024),
    )(gathered, *factors)


def shift(value, axis, step):
    size = lax.axis_size(axis)
    return lax.ppermute(value, axis, [(i, (i + step) % size) for i in range(size)])


def ring(value, cut):
    behind = shift(value, "x", 1)
    ahead = shift(value, "x", 3)
    far_up = shift(behind[:cut], "x", 1)
    far_down = shift(ahead[cut:], "x", 3)
    return [behind, ahead, far_up, far_down]


def spread(value, cut):
    other = shift(value, "h", 1)
    return [value] + ring(value, cut) + [other] + ring(other, cut)


def total_over_all(value):
    for axis in ("c", "x", "y", "l", "h"):
        parts = [shift(value, axis, step) for step in range(1, lax.axis_size(axis))]
        for part in parts:
            value = value + part
    return value


def per_device(
    prompt_states,
    decode_states,
    norm_gain,
    query_bias,
    value_bias,
    w_query,
    w_key,
    w_value,
    w_out,
    targets,
    lengths,
    seeds,
):
    member_id = lax.axis_index(MEMBER)
    tensor_id = lax.axis_index(TENSOR)
    x_id = lax.axis_index("x")
    h_id = lax.axis_index("h")
    seed = seeds[member_id]
    place = jnp.stack(
        [member_id, tensor_id, lengths[2 * member_id], lengths[2 * member_id + 1]]
    ).astype(jnp.int32)
    order = jnp.stack(
        [((x_id + step) % 4) * 2 + (h_id + flip) % 2
         for step, flip in ((0, 0), (0, 1), (3, 0), (1, 0), (3, 1), (1, 1), (2, 0), (2, 1))]
    ).astype(jnp.int32)

    qkv = lax.all_gather(
        jnp.concatenate([w_query, w_key, w_value], axis=1), MEMBER, axis=0, tiled=True
    )
    moves = [
        (m * N_TENSOR + t, (t * 4 + m % 4) * N_TENSOR + m // 4)
        for m in range(N_MEMBER)
        for t in range(N_TENSOR)
    ]
    out_piece = lax.ppermute(w_out.T, MEMBER + TENSOR, moves)
    out_weights = lax.all_gather(out_piece, MEMBER, axis=0, tiled=True)

    payload = jnp.concatenate(
        [decode_states, prompt_states, jnp.broadcast_to(norm_gain[None, :], (PAD, SHARE))], axis=0
    )
    cut = 384
    pieces = spread(payload, cut)

    def squares(value):
        value = value.astype(F32)
        return jnp.sum(value * value, axis=1, keepdims=True)

    sums = jnp.zeros((ROWS, 1), F32)
    for first in (0, 5):
        own, behind, ahead, up, down = pieces[first : first + 5]
        sums = sums + squares(own[:ROWS]) + squares(behind[:ROWS]) + squares(ahead[:ROWS])
        sums = sums + jnp.concatenate([squares(up), squares(down[: ROWS - cut])], axis=0)
    scale = lax.rsqrt(sums * (1.0 / D) + 1e-06)

    row_ids = jnp.arange(D, dtype=jnp.int32)
    query_cols = tensor_id * QUERY_WIDTH + jnp.arange(QUERY_WIDTH, dtype=jnp.int32)
    pair_cols = tensor_id * HEAD_DIM + jnp.arange(HEAD_DIM, dtype=jnp.int32)
    own_rows = member_id * PIECE + jnp.arange(PIECE, dtype=jnp.int32)
    table_left = tall_table(seed, 0, 3, row_ids, 128)
    table_right = jnp.zeros((128, ALL_WIDTH), BF16)
    table_right = table_right.at[:RANK, :QUERY_WIDTH].set(wide_table(seed, 4, query_cols))
    table_right = table_right.at[RANK : 2 * RANK, QUERY_WIDTH : QUERY_WIDTH + HEAD_DIM].set(
        wide_table(seed, 5, pair_cols)
    )
    table_right = table_right.at[2 * RANK : 3 * RANK, QUERY_WIDTH + HEAD_DIM :].set(
        wide_table(seed, 6, pair_cols)
    )
    out_left = tall_table(seed, 3, 1, row_ids, 128)
    out_right = jnp.zeros((128, SHARE), BF16).at[:RANK].set(wide_table(seed, 7, query_cols))
    factors = (
        all_left(seeds, 0, own_rows),
        all_right(seeds, 4, query_cols),
        all_left(seeds, 1, own_rows),
        all_right(seeds, 5, pair_cols),
        all_left(seeds, 2, own_rows),
        all_right(seeds, 6, pair_cols),
        all_left(seeds, 3, query_cols),
        all_right(seeds, 7, own_rows),
    )

    mixed = attention(
        order,
        scale,
        query_bias[None, :],
        value_bias[None, :],
        table_right,
        table_left,
        qkv,
        pieces,
    )
    shares = spread(mixed, DEC)
    errors = output_errors(order, place, out_weights, out_left, out_right, targets, shares)
    gathered = total_over_all(errors)
    fitness, grad_query, grad_key, grad_value, grad_out = gradients(gathered, factors)
    return (fitness[0, : 2 * N_MEMBER], grad_query, grad_key, grad_value, grad_out)


def solution(mesh):
    fine = Mesh(mesh.devices.reshape(4, 4, 2, 4, 2), ("y", "l", "c", "x", "h"))
    both = P(MEMBER, TENSOR)
    turned = P(TENSOR, MEMBER)
    line = P(TENSOR)
    return jax.shard_map(
        per_device,
        mesh=fine,
        in_specs=(both, both, line, line, line, both, both, both, turned, both, P(), P()),
        out_specs=(P(), both, both, both, turned),
        check_vma=False,
    )
```
